32 devices in a mesh: tm: 8 (over y, x, core), row: 4 (over z).
Axes of the slice: x: 2, y: 2, z: 4, core: 2. Of those that a mesh axis runs over, the one named last changes fastest.
Arguments:
- pred_cov: bfloat16 [8, 1536, 1536], P('tm', 'row'), may hold values from -0.8 to 3.3, as said below
- cross: float32 [8, 1536, 1536], P('tm', 'row'), may hold values from -0.9 to 3.2
- filt_mean: float32 [8, 1536], P('tm', 'row'), may hold values from -6 to 6
- pred_mean: float32 [8, 1536], P('tm', 'row'), may hold values from -6 to 6
- next_smoothed: float32 [1536], P('row'), may hold values from -6 to 6
Outputs:
- smoothed: float32 [8, 1536], P('tm', 'row')
- gains: float32 [8, 1536, 1536], P('tm', 'row')
The draws below stay inside these ranges and needn't reach their ends.
Inputs may be any that keep to these rules, and one draw needn't show every extreme that they name: `pred_cov`: each of the 8 matrices of size 1536 x 1536 is symmetric positive definite.
All inputs are finite; a program needn't handle non-finite values.
Results may differ from the reference program's by a relative error of at most 0.0003.
Values may be sent and summed in bfloat16 or wider, within the bound.
A program may use at most 128 MiB of HBM per device.

```python
import math
import jax
import jax.numpy as jnp
from jax import lax

MODEL_DIMENSION = 1536
HORIZON_LENGTH = 8


def shared_scales(key):
    principal_values = jax.random.uniform(jax.random.fold_in(key, 101), (HORIZON_LENGTH, MODEL_DIMENSION), jnp.float32, 1.2, 2.0)
    spans = jnp.exp(jax.random.uniform(jax.random.fold_in(key, 102), (MODEL_DIMENSION,), jnp.float32, math.log(2.0), math.log(4.0 * HORIZON_LENGTH)))
    retain_markers = jnp.exp(-1.0 / spans)
    batch_clusters = jnp.where(jax.random.uniform(jax.random.fold_in(key, 103), (HORIZON_LENGTH, MODEL_DIMENSION), jnp.float32) < 0.0625, 0.6, 1.0)
    return (principal_values, retain_markers[None, :] * batch_clusters)


def identity_mask():
    rows = lax.broadcasted_iota(jnp.int32, (MODEL_DIMENSION, MODEL_DIMENSION), 0)
    cols = lax.broadcasted_iota(jnp.int32, (MODEL_DIMENSION, MODEL_DIMENSION), 1)
    return (rows == cols)[None, :, :]


def link_coupling():
    rows = lax.broadcasted_iota(jnp.int32, (MODEL_DIMENSION, MODEL_DIMENSION), 0)
    cols = lax.broadcasted_iota(jnp.int32, (MODEL_DIMENSION, MODEL_DIMENSION), 1)
    link_spacing = jnp.abs(rows // 2 - cols // 2).astype(jnp.float32)
    wide_reach = max(MODEL_DIMENSION / 8.0, 1.0)
    kernel = 0.25 * jnp.exp(-link_spacing / 2.0) + 2.0 / wide_reach * jnp.exp(-link_spacing / wide_reach)
    same_kind = rows % 2 == cols % 2
    return jnp.where(same_kind, 1.0, -0.6) * kernel


def full_covariance(key):
    principal_values, retain_markers = shared_scales(key)
    noise = jax.random.uniform(jax.random.fold_in(key, 104), (HORIZON_LENGTH, MODEL_DIMENSION, MODEL_DIMENSION), jnp.float32, -0.5, 0.5) / MODEL_DIMENSION
    symmetric = 0.5 * (noise + jnp.swapaxes(noise, 1, 2))
    loading = jnp.exp(jax.random.uniform(jax.random.fold_in(key, 106), (HORIZON_LENGTH, MODEL_DIMENSION), jnp.float32, math.log(0.5), math.log(1.5)))
    smooth = loading[:, :, None] * loading[:, None, :] * link_coupling()[None, :, :]
    full = smooth + jnp.where(identity_mask(), principal_values[:, :, None], symmetric)
    process_share = jax.random.uniform(jax.random.fold_in(key, 107), (HORIZON_LENGTH, MODEL_DIMENSION), jnp.float32, 0.1, 0.4)
    process_noise = process_share * principal_values
    return (full, retain_markers, process_noise)


def draw_pred_cov(key, part):
    full, retain_markers, process_noise = full_covariance(key)
    return full.astype(jnp.bfloat16)


def draw_cross(key, part):
    full, retain_markers, process_noise = full_covariance(key)
    noise = jax.random.normal(jax.random.fold_in(key, 105), (HORIZON_LENGTH, MODEL_DIMENSION, MODEL_DIMENSION), jnp.float32) * 0.01
    reduced = full - jnp.where(identity_mask(), process_noise[:, :, None], 0.0)
    return retain_markers[:, :, None] * reduced + noise


def draw_pred_mean(key, part):
    values = jax.random.normal(jax.random.fold_in(key, 201), (HORIZON_LENGTH, MODEL_DIMENSION), jnp.float32)
    return jnp.clip(values, -6.0, 6.0)


def block_levels(rng, shape, pieces, smallest, high):
    loudness, own = 1.0, jax.random.fold_in(rng, 6)
    for dim, shards_of in pieces:
        draws = jnp.exp(jax.random.uniform(jax.random.fold_in(own, dim), (shards_of,), jnp.float32, smallest / len(pieces), high / len(pieces)))
        loudness = loudness * jnp.repeat(draws, shape[dim] // shards_of).reshape([-1 if axis == dim else 1 for axis in range(len(shape))])
    return loudness


def bell_draw(stream_key, dims, spread, limit, pieces=(), kind=jnp.bfloat16):
    entries = spread * jax.random.normal(stream_key, dims, jnp.float32)
    if pieces:
        entries = entries * block_levels(stream_key, dims, pieces, -0.22, 0.18)
    return jnp.clip(entries, -limit, limit).astype(kind)


def setup_inputs(seed: int = 0) -> dict:
    arg_keys = jax.random.split(jax.random.key(seed), 6)
    pred_cov = draw_pred_cov(jax.random.fold_in(arg_keys[5], 71), 0)
    cross = draw_cross(jax.random.fold_in(arg_keys[5], 71), 0)
    filt_mean = bell_draw(arg_keys[2], (HORIZON_LENGTH, MODEL_DIMENSION), 1.0, 6.0, ((0, 8), (1, 4)), jnp.float32)
    pred_mean = draw_pred_mean(jax.random.fold_in(arg_keys[5], 71), 0)
    next_smoothed = bell_draw(arg_keys[4], (MODEL_DIMENSION,), 1.0, 6.0, ((0, 4),), jnp.float32)
    return dict(pred_cov=pred_cov, cross=cross, filt_mean=filt_mean, pred_mean=pred_mean, next_smoothed=next_smoothed)


def one_gain(pair):
    cov, part = pair
    cholesky_factor = jnp.linalg.cholesky(cov.astype(jnp.float32))
    return jax.scipy.linalg.cho_solve((cholesky_factor, True), part.T).T

def reference(pred_cov, cross, filt_mean, pred_mean, next_smoothed):
    gains = lax.map(one_gain, (pred_cov, cross))

    def backward(later, items):
        gain, mean_f, mean_p = items
        now = mean_f + jnp.dot(gain.astype(jnp.float32), (later - mean_p).astype(jnp.float32), precision=lax.Precision.HIGHEST, preferred_element_type=jnp.float32)
        return (now, now)
    _, smoothed = lax.scan(backward, next_smoothed, (gains, filt_mean, pred_mean), reverse=True)
    return (smoothed, gains)
```

```python
import functools

import jax
import jax.numpy as jnp
from jax import lax
from jax.experimental import pallas as pl
from jax.experimental.pallas import tpu as pltpu
from jax.sharding import PartitionSpec as P

finest = lax.Precision.HIGHEST
LANES = 128
CHUNK = 16
MOST_TURNS = 48
TOLERANCE = 2.0**-21


def from_behind(array, axis, by):
    peers = lax.axis_size(axis)
    pairs = [(i, i + by) for i in range(peers) if 0 <= i + by < peers]
    return lax.ppermute(array, axis, pairs)


def matvec(matrix, vector):
    return jnp.dot(matrix, vector, precision=finest, preferred_element_type=jnp.float32)


def folded(values):
    return sum(values[:, i : i + LANES] for i in range(0, values.shape[1], LANES))


def ratio(top, bottom):
    fine = bottom > 0.0
    return jnp.where(fine, top / jnp.where(fine, bottom, 1.0), 0.0)


def refine_kernel(cov, cross, gain, state, rest, image, way, partial, scale):
    rows, width = cross.shape
    tile = 256 if width % 256 == 0 else width
    chunks = rows // CHUNK
    unroll = 4 if chunks % 4 == 0 else 1

    def each_chunk(body):
        def step(i, carry):
            body(pl.ds(pl.multiple_of(i * CHUNK, CHUNK), CHUNK))
            return carry

        lax.fori_loop(0, chunks, step, 0, unroll=unroll)

    def begin(at):
        start = cross[at, :]
        rest[at, :] = start
        way[at, :] = start.astype(jnp.bfloat16)
        gain[at, :] = jnp.zeros_like(start)
        partial[at, :] = folded(start * start)

    each_chunk(begin)
    first = jnp.sum(partial[...], axis=1, keepdims=True)
    bound = first * (TOLERANCE * TOLERANCE)

    def excess(squares):
        return jnp.max(squares - bound)

    def advance(carry):
        turn, squares, _ = carry
        partial[...] = jnp.zeros_like(partial)

        def column(j, unused):
            at = pl.ds(pl.multiple_of(j * tile, tile), tile)
            product = jnp.dot(way[...], cov[:, at], preferred_element_type=jnp.float32)
            image[:, at] = product
            partial[...] += folded(product * way[:, at].astype(jnp.float32))
            return unused

        lax.fori_loop(0, width // tile, column, 0)
        length = ratio(squares, jnp.sum(partial[...], axis=1, keepdims=True))
        scale[...] = jnp.broadcast_to(length, scale.shape)

        def move(at):
            by = scale[at, :][:, :1]
            gain[at, :] += by * way[at, :].astype(jnp.float32)
            left = rest[at, :] - by * image[at, :]
            rest[at, :] = left
            partial[at, :] = folded(left * left)

        each_chunk(move)
        fresh = jnp.sum(partial[...], axis=1, keepdims=True)
        scale[...] = jnp.broadcast_to(ratio(fresh, squares), scale.shape)

        def turn_way(at):
            by = scale[at, :][:, :1]
            ahead = rest[at, :] + by * way[at, :].astype(jnp.float32)
            way[at, :] = ahead.astype(jnp.bfloat16)

        each_chunk(turn_way)
        return turn + 1, fresh, excess(fresh)

    def unfinished(carry):
        turn, _, over = carry
        return jnp.logical_and(turn < MOST_TURNS, jnp.logical_not(over <= 0.0))

    _, _, over = lax.while_loop(unfinished, advance, (jnp.int32(0), first, excess(first)))
    state[0, 0] = jnp.where(over <= 0.0, 1, 0)


def refine(cov, cross):
    rows, width = cross.shape
    vmem = pl.BlockSpec(memory_space=pltpu.VMEM)
    return pl.pallas_call(
        refine_kernel,
        out_shape=(
            jax.ShapeDtypeStruct((rows, width), jnp.float32),
            jax.ShapeDtypeStruct((1, 1), jnp.int32),
        ),
        in_specs=[vmem, vmem],
        out_specs=(vmem, pl.BlockSpec(memory_space=pltpu.SMEM)),
        scratch_shapes=[
            pltpu.VMEM((rows, width), jnp.float32),
            pltpu.VMEM((rows, width), jnp.float32),
            pltpu.VMEM((rows, width), jnp.bfloat16),
            pltpu.VMEM((rows, LANES), jnp.float32),
            pltpu.VMEM((rows, LANES), jnp.float32),
        ],
        compiler_params=pltpu.CompilerParams(vmem_limit_bytes=48 * 2**20),
        cost_estimate=pl.CostEstimate(
            flops=32 * rows * width * width, bytes_accessed=16 * rows * width, transcendentals=0
        ),
    )(cov, cross)


def direct(cov, cross):
    cholesky_factor = jnp.linalg.cholesky(cov.astype(jnp.float32))
    return jax.scipy.linalg.cho_solve((cholesky_factor, True), cross.T).T


def backward_kernel(steps, peers, gain, mean_f, mean_p, ahead, out, means, later, mean_sent, mean_came, sent, came):
    t = lax.axis_index("tm")
    me = lax.axis_index("row")
    width = mean_f.shape[1]
    final = t == steps - 1

    def other(k):
        return lax.rem(me + k, peers)

    def greet(step, row):
        pl.semaphore_signal(
            pltpu.get_barrier_semaphore(),
            inc=1,
            device_id=(step, row),
            device_id_type=pl.DeviceIdType.MESH,
        )

    for k in range(1, peers):
        greet(t, other(k))

    @pl.when(t > 0)
    def _():
        for k in range(peers):
            greet(t - 1, other(k))

    @pl.when(jnp.logical_not(final))
    def _():
        for k in range(peers):
            greet(t + 1, other(k))

    greeters = jnp.where(jnp.logical_or(t == 0, final), 2 * peers - 1, 3 * peers - 1)
    pl.semaphore_wait(pltpu.get_barrier_semaphore(), greeters)

    def copy(source, target, slot, sends, comes, k, step, row):
        return pltpu.make_async_remote_copy(
            src_ref=source,
            dst_ref=target.at[slot],
            send_sem=sends.at[k],
            recv_sem=comes.at[slot],
            device_id=(step, row),
            device_id_type=pl.DeviceIdType.MESH,
        )

    for k in range(1, peers):
        copy(mean_p, means, me, mean_sent, mean_came, k, t, other(k)).start()
    means[pl.ds(me, 1)] = mean_p[...][None]

    @pl.when(final)
    def _():
        for k in range(1, peers):
            copy(ahead, later, me, sent, came, k, t, other(k)).start()
        later[pl.ds(me, 1)] = ahead[...][None]
        for k in range(1, peers):
            copy(ahead, later, me, sent, came, k, t, other(k)).wait_send()

    for k in range(1, peers):
        copy(mean_p, means, me, mean_sent, mean_came, k, t, other(k)).wait_send()
    for k in range(1, peers):
        copy(mean_p, means, other(k), mean_sent, mean_came, k, t, other(k)).wait_recv()

    @pl.when(jnp.logical_not(final))
    def _():
        copy(ahead, later, me, sent, came, 0, t + 1, me).wait_recv()

    for k in range(1, peers):
        copy(ahead, later, other(k), sent, came, k, t, other(k)).wait_recv()

    total = jnp.zeros((width, LANES), jnp.float32)
    for j in range(peers):
        innovation = later[j] - means[j]
        for i in range(0, width, LANES):
            total += gain[:, j * width + i : j * width + i + LANES] * innovation[:, i : i + LANES]
    out[...] = mean_f[...] + jnp.sum(total.T, axis=0, keepdims=True)

    @pl.when(t > 0)
    def _():
        for k in range(peers):
            copy(out, later, me, sent, came, k, t - 1, other(k)).start()
        for k in range(peers):
            copy(out, later, me, sent, came, k, t - 1, other(k)).wait_send()


def backward(gain, mean_f, mean_p, ahead):
    steps, peers = lax.axis_size("tm"), lax.axis_size("row")
    width = mean_f.shape[1]
    vmem = pl.BlockSpec(memory_space=pltpu.VMEM)
    return pl.pallas_call(
        functools.partial(backward_kernel, steps, peers),
        out_shape=jax.ShapeDtypeStruct((1, width), jnp.float32),
        in_specs=[vmem] * 4,
        out_specs=vmem,
        scratch_shapes=[
            pltpu.VMEM((peers, 1, width), jnp.float32),
            pltpu.VMEM((peers, 1, width), jnp.float32),
            pltpu.SemaphoreType.DMA((peers,)),
            pltpu.SemaphoreType.DMA((peers,)),
            pltpu.SemaphoreType.DMA((peers,)),
            pltpu.SemaphoreType.DMA((peers,)),
        ],
        compiler_params=pltpu.CompilerParams(
            collective_id=1, has_side_effects=True, vmem_limit_bytes=32 * 2**20
        ),
        cost_estimate=pl.CostEstimate(
            flops=2 * width * width * peers, bytes_accessed=4 * width * width * peers, transcendentals=0
        ),
    )(gain, mean_f, mean_p, ahead)


def backward_by_collectives(gain, mean_f, mean_p, ahead):
    steps = lax.axis_size("tm")
    final = lax.axis_index("tm") == steps - 1

    def advance(turn, state):
        later = from_behind(state, "tm", -1)
        later = jnp.where(final, ahead[0], later)
        dispersion = lax.all_gather(later - mean_p[0], "row", axis=0, tiled=True)
        return mean_f[0] + matvec(gain, dispersion)

    return lax.fori_loop(0, steps, advance, jnp.zeros_like(mean_f[0]))[None, :]


def per_device(pred_cov, cross, filt_mean, pred_mean, next_smoothed):
    whole_cov = lax.all_gather(pred_cov, "row", axis=1, tiled=True)[0]
    found, state = refine(whole_cov, cross[0])
    gain = lax.cond(
        state[0, 0] == 1, lambda cov, part, found: found, lambda cov, part, found: direct(cov, part),
        whole_cov, cross[0], found,
    )
    aligned = filt_mean.shape[1] % LANES == 0
    sweep = backward if aligned else backward_by_collectives
    smoothed = sweep(gain, filt_mean, pred_mean, next_smoothed[None, :])
    return (smoothed, gain[None, :, :])


def solution(mesh):
    in_specs = (
        P("tm", "row", None),
        P("tm", "row", None),
        P("tm", "row"),
        P("tm", "row"),
        P("row"),
    )
    out_specs = (P("tm", "row"), P("tm", "row", None))
    return jax.shard_map(
        per_device, mesh=mesh, in_specs=in_specs, out_specs=out_specs, check_vma=False
    )
```
